512 devices in a mesh: dp: 16 (over z, core), ctx: 32 (over x, y).
Axes of the slice: x: 4, y: 8, z: 8, core: 2. Of those that a mesh axis runs over, the one named last changes fastest.
Arguments:
- frames: bfloat16 [512, 2, 512, 512], P(('dp', 'ctx')), parts along dimension 0, may hold values from -6 to 6
- episode_lengths: int32 [1024], P('dp'), parts along dimension 0, may hold values from 1 to 1024, 32768 in all
- w_qkv: bfloat16 [512, 1536], replicated, may hold values from -1 to 1
- w_out: bfloat16 [512, 512], replicated, may hold values from -0.25 to 0.25
Outputs:
- attended: bfloat16 [512, 2, 512, 512], P(('dp', 'ctx')), parts along dimension 0
The draws below stay inside these ranges and needn't reach their ends.
There are 16 independent parts, one for each index of `dp`. The reference program is written for one: setup_inputs(seed, part) draws one part's arguments, and reference() takes and returns one part's arrays. A program takes and returns all parts, laid end to end along the dimension named above; an argument that names none is the same for every part. Nothing has to cross between parts.
Inputs may be any that keep to these rules, and one draw needn't show every extreme that they name: `episode_lengths`: the lengths sum to 32768; the longest is exactly 1024 tokens.
All inputs are finite; a program needn't handle non-finite values.
Results may differ from the reference program's by a relative error of at most 0.0082.
Values may be sent and summed in bfloat16 or wider, within the bound.
A program may use at most 64 MiB of HBM per device.

```python
import math
import jax
import jax.numpy as jnp
import numpy as np
from jax import lax

D = 512
HEADS = 4
HEAD_DIM = 128
CH = 512
WIN = 2
SEQ = 32768
EPI_MAX = 1024
EPISODES = 64
N_CTX = 32


def draw_frames(key, part):
    shape = (N_CTX, 2, CH, D)
    noise = jax.random.truncated_normal(key, -4.0, 4.0, shape, jnp.float32)
    return noise.astype(jnp.bfloat16)


def draw_w_qkv(key, part):
    base = jax.random.truncated_normal(key, -4.0, 4.0, (D, 3 * D), jnp.float32) * D ** (-0.5)
    return base.astype(jnp.bfloat16)


def length_profile(count, total, limit, lean):
    portions = [(1 << 20) // math.isqrt(standing ** lean) + 1 for standing in range(2, count + 1)]
    surplus, given = total - limit - (count - 1), [1] * (count - 1)
    while surplus > 0:
        movable = [i for i in range(count - 1) if given[i] < limit]
        mass, budget = sum([portions[i] for i in movable]), surplus
        for i in movable:
            extra = min(limit - given[i], max(1, budget * portions[i] // mass), surplus)
            given[i] = given[i] + extra
            surplus = surplus - extra
    return np.array([limit] + given)


def ragged(own_key, number_of, total, reach, slope):
    if number_of == 2:
        one = jax.random.randint(own_key, (), max(1, total - reach), min(reach, total - 1) + 1)
        return jnp.stack([one, total - one])
    lengths = jnp.asarray(length_profile(number_of, total, reach, slope), jnp.int32)
    twos = (number_of - 1) // 2
    source_of, sink = lengths[1:1 + 2 * twos:2], lengths[2:2 + 2 * twos:2]
    margin = jnp.minimum(source_of - 1, reach - sink)
    moved = jax.random.randint(jax.random.fold_in(own_key, 1), (twos,), 0, 1 << 20) % (margin + 1)
    lengths = lengths.at[1:1 + 2 * twos:2].set(source_of - moved).at[2:2 + 2 * twos:2].set(sink + moved)
    return lengths[jax.random.permutation(jax.random.fold_in(own_key, 2), number_of)]


def scatter_about(rng, dims, deviation, most, held_as=jnp.bfloat16):
    return jnp.clip(deviation * jax.random.normal(rng, dims, jnp.float32), -most, most).astype(held_as)


def setup_inputs(seed: int = 0, part: int = 0) -> dict:
    arg_keys = jax.random.split(jax.random.key(seed), 5)
    part_keys = jax.random.split(jax.random.fold_in(arg_keys[4], part), 5)
    frames = draw_frames(jax.random.fold_in(jax.random.fold_in(arg_keys[4], part), 71), part)
    episode_lengths = ragged(part_keys[1], EPISODES, SEQ, EPI_MAX, 2).astype(jnp.int32)
    w_qkv = draw_w_qkv(jax.random.fold_in(arg_keys[4], 71), part)
    w_out = scatter_about(arg_keys[3], (D, D), D ** -0.5, 0.25)
    return {"frames": frames, "episode_lengths": episode_lengths, "w_qkv": w_qkv, "w_out": w_out}


def normalize(rows):
    wide = rows.astype(jnp.float32)
    factor = lax.rsqrt(lax.optimization_barrier(jnp.mean(wide * wide, axis=-1, keepdims=True)) + 1e-06)
    return (wide * factor).astype(jnp.bfloat16)

def episode_start(positions, episode_lengths):
    ends = jnp.cumsum(episode_lengths).astype(jnp.int32)
    passed = (ends[None, :] <= positions[:, None]).astype(jnp.int32)
    return lax.optimization_barrier(jnp.sum(passed * episode_lengths[None, :], axis=1)).astype(jnp.int32)

def attend(queries, keys, values, query_pos, key_pos, starts):
    allowed = (key_pos[None, :] <= query_pos[:, None]) & (key_pos[None, :] >= starts[:, None])
    outputs = []
    for head in range(HEADS):
        low = head * HEAD_DIM
        high = low + HEAD_DIM
        scores = lax.dot_general(queries[:, low:high], keys[:, low:high], (((1,), (1,)), ((), ())), preferred_element_type=jnp.float32)
        scores = scores * HEAD_DIM ** (-0.5)
        scores = jnp.where(allowed, scores, -jnp.inf)
        peak = lax.optimization_barrier(jnp.max(scores, axis=1, keepdims=True))
        weights = jnp.exp(scores - peak)
        totals = lax.optimization_barrier(jnp.sum(weights, axis=1, keepdims=True))
        mixed = jnp.dot(weights.astype(jnp.bfloat16), values[:, low:high], preferred_element_type=jnp.float32) / totals
        outputs.append(mixed)
    return jnp.concatenate(outputs, axis=1).astype(jnp.bfloat16)

def reference(frames, episode_lengths, w_qkv, w_out):
    lower = frames[:, 0]
    upper = frames[::-1, 1]
    tokens = jnp.concatenate([lower, upper], axis=0).reshape(SEQ, D)
    normed = normalize(tokens)
    projected = jnp.dot(normed, w_qkv, preferred_element_type=jnp.float32).astype(jnp.bfloat16)
    queries = projected[:, :D]
    padding = jnp.zeros((WIN * CH, D), jnp.bfloat16)
    keys = jnp.concatenate([padding, projected[:, D:2 * D]], axis=0)
    values = jnp.concatenate([padding, projected[:, 2 * D:]], axis=0)
    positions = jnp.arange(SEQ, dtype=jnp.int32)
    starts = episode_start(positions, episode_lengths)

    def block(index):
        first = (index * CH).astype(jnp.int32)
        query_rows = lax.dynamic_slice_in_dim(queries, first, CH, 0)
        key_rows = lax.dynamic_slice_in_dim(keys, first, (WIN + 1) * CH, 0)
        value_rows = lax.dynamic_slice_in_dim(values, first, (WIN + 1) * CH, 0)
        block_starts = lax.dynamic_slice_in_dim(starts, first, CH, 0)
        query_pos = first + jnp.arange(CH, dtype=jnp.int32)
        key_pos = first - WIN * CH + jnp.arange((WIN + 1) * CH, dtype=jnp.int32)
        mixed = attend(query_rows, key_rows, value_rows, query_pos, key_pos, block_starts)
        return jnp.dot(mixed, w_out, preferred_element_type=jnp.float32).astype(jnp.bfloat16)
    result = lax.map(block, jnp.arange(2 * N_CTX, dtype=jnp.int32))
    return jnp.stack([result[:N_CTX], result[N_CTX:][::-1]], axis=1)
```

```python
import functools

import jax
import jax.numpy as jnp
from jax import lax
from jax.experimental import pallas as pl
from jax.experimental.pallas import tpu as pltpu
from jax.sharding import PartitionSpec as P

HEADS = 4
HEAD_DIM = 128
WIN = 2
GROUP = 512
WIDTH = 512
CHUNK = 256
CHUNKS = GROUP // CHUNK
FAR = -(2.0**100)
RATE = HEAD_DIM ** (-0.5) * 1.4426950408889634


def normalize(rows):
    wide = rows.astype(jnp.float32)
    factor = lax.rsqrt(jnp.mean(wide * wide, axis=-1, keepdims=True) + 1e-06)
    return (wide * factor).astype(jnp.bfloat16)


def episode_bounds(lengths):
    count = lengths.shape[1]
    row = lax.broadcasted_iota(jnp.int32, (count, count), 0)
    col = lax.broadcasted_iota(jnp.int32, (count, count), 1)
    spread = jnp.broadcast_to(lengths.astype(jnp.float32), (count, count))
    column = jnp.sum(jnp.where(row == col, spread, 0.0), axis=1, keepdims=True)
    row = lax.broadcasted_iota(jnp.int32, (count, 128), 0)
    col = lax.broadcasted_iota(jnp.int32, (count, 128), 1)
    ends = jnp.sum(jnp.where(row <= col, column, 0.0), axis=0, keepdims=True)
    starts = jnp.sum(jnp.where(row < col, column, 0.0), axis=0, keepdims=True)
    return starts, ends


def kernel(
    count,
    frames,
    lengths,
    w_qkv_hbm,
    w_out_hbm,
    out,
    own,
    landed,
    w_qkv,
    w_out,
    queries,
    pairs,
    peaks,
    sums,
    result,
    bounds,
    load_sem,
    store_sem,
    send_sem,
    recv_sem,
):
    place = lax.axis_index("ctx")
    right = lax.rem(place + 1, count)
    left = lax.rem(place + count - 1, count)
    first_place = place == 0
    last_place = place == count - 1

    barrier = pltpu.get_barrier_semaphore()
    for neighbour in (left, right):
        pl.semaphore_signal(
            barrier, inc=1, device_id={"ctx": neighbour}, device_id_type=pl.DeviceIdType.MESH
        )

    loads = [
        pltpu.make_async_copy(frames.at[0], own, load_sem.at[0]),
        pltpu.make_async_copy(w_qkv_hbm, w_qkv, load_sem.at[1]),
        pltpu.make_async_copy(w_out_hbm, w_out, load_sem.at[2]),
    ]
    for load in loads:
        load.start()

    def rows(chunk):
        return pl.ds(chunk * CHUNK, CHUNK)

    def link(half, stage, chunk):
        source = frames.at[0, half, rows(chunk)] if stage == 0 else landed.at[half, 0, rows(chunk)]
        return pltpu.make_async_remote_copy(
            src_ref=source,
            dst_ref=landed.at[half, stage, rows(chunk)],
            send_sem=send_sem.at[half, stage, chunk],
            recv_sem=recv_sem.at[half, stage, chunk],
            device_id={"ctx": right if half == 0 else left},
            device_id_type=pl.DeviceIdType.MESH,
        )

    def inside(stage, chunk):
        source = frames.at[0, 0, rows(chunk)] if stage == 0 else landed.at[0, 0, rows(chunk)]
        return pltpu.make_async_copy(
            source, landed.at[1, stage, rows(chunk)], recv_sem.at[1, stage, chunk]
        )

    def send(stage, chunk):
        link(0, stage, chunk).start()

        @pl.when(jnp.logical_not(first_place))
        def _():
            link(1, stage, chunk).start()

        @pl.when(last_place)
        def _():
            inside(stage, chunk).start()

    def arrive(stage, chunk):
        link(0, stage, chunk).wait_recv()

        @pl.when(jnp.logical_not(last_place))
        def _():
            link(1, stage, chunk).wait_recv()

        @pl.when(last_place)
        def _():
            inside(stage, chunk).wait()

    def sent(stage, chunk):
        link(0, stage, chunk).wait_send()

        @pl.when(jnp.logical_not(first_place))
        def _():
            link(1, stage, chunk).wait_send()

    order = list(range(CHUNKS))[::-1]

    starts, ends = episode_bounds(lengths[...])
    bounds[0:1, :] = starts
    bounds[1:2, :] = ends

    pl.semaphore_wait(barrier, 2)
    for chunk in order:
        send(0, chunk)

    def marks(first, number, inner, outer):
        at = (first + lax.broadcasted_iota(jnp.int32, (number, 128), 0)).astype(jnp.float32)
        within = (at >= bounds[0:1, :]) & (at < bounds[1:2, :])
        return jnp.where(within, inner, outer).astype(jnp.bfloat16)

    def lanes(head):
        return slice(head * 128, head * 128 + 128)

    def wide_lanes(head):
        return slice(head * 256, head * 256 + 256)

    ones = jnp.ones((1, 128), jnp.bfloat16)

    def attend(half, tile, keys, values, key_marks, diagonal, fresh):
        span = pl.ds(tile * CHUNK, CHUNK)
        number = keys.shape[0]
        if diagonal:
            query_at = tile * CHUNK + lax.broadcasted_iota(jnp.int32, (CHUNK, number), 0)
            key_at = lax.broadcasted_iota(jnp.int32, (CHUNK, number), 1)
            behind = key_at <= query_at
        ones_column = jnp.broadcast_to(ones, (number, 128))
        for head in range(HEADS):
            key_part = jnp.concatenate([keys[:, lanes(head)], key_marks], axis=1)
            value_part = jnp.concatenate([values[:, lanes(head)], ones_column], axis=1)
            scores = lax.dot_general(
                queries[half, span, wide_lanes(head)],
                key_part,
                (((1,), (1,)), ((), ())),
                preferred_element_type=jnp.float32,
            )
            if diagonal:
                scores = jnp.where(behind, scores, FAR)
            peak = jnp.max(scores, axis=1, keepdims=True)
            if fresh:
                weights = jnp.exp2((scores - peak) * RATE).astype(jnp.bfloat16)
                sums[half, span, wide_lanes(head)] = jnp.dot(
                    weights, value_part, preferred_element_type=jnp.float32
                )
                peaks[half, span, lanes(head)] = jnp.broadcast_to(peak, (CHUNK, 128))
            else:
                before = peaks[half, span, lanes(head)]
                now = jnp.maximum(before, peak)
                scale = jnp.exp2((before - now) * RATE)
                weights = jnp.exp2((scores - now[:, :1]) * RATE).astype(jnp.bfloat16)
                sums[half, span, wide_lanes(head)] = sums[half, span, wide_lanes(head)] * jnp.concatenate(
                    [scale, scale], axis=1
                ) + jnp.dot(weights, value_part, preferred_element_type=jnp.float32)
                peaks[half, span, lanes(head)] = now

    def block_first(half):
        return GROUP * (place + half * (2 * count - 1 - 2 * place))

    loads[0].wait()
    loads[1].wait()

    def own_half(half, carry):
        base = block_first(half)
        for tile in range(CHUNKS):
            span = slice(tile * CHUNK, tile * CHUNK + CHUNK)
            normed = normalize(own[half, span])
            query_part = jnp.dot(
                normed, w_qkv[:, :WIDTH], preferred_element_type=jnp.float32
            ).astype(jnp.bfloat16)
            query_marks = marks(base + tile * CHUNK, CHUNK, FAR, 0.0)
            for head in range(HEADS):
                queries[half, span, head * 256 : head * 256 + 128] = query_part[:, lanes(head)]
                queries[half, span, head * 256 + 128 : head * 256 + 256] = query_marks
            pairs[span] = jnp.dot(
                normed, w_qkv[:, WIDTH:], preferred_element_type=jnp.float32
            ).astype(jnp.bfloat16)
        for tile in range(CHUNKS):
            number = (tile + 1) * CHUNK
            attend(
                half,
                tile,
                pairs[:number, :WIDTH],
                pairs[:number, WIDTH:],
                marks(base, number, 0.0, 1.0),
                True,
                True,
            )
        return carry

    lax.fori_loop(0, 2, own_half, 0)

    for stage in range(WIN):
        for chunk in order:
            arrive(stage, chunk)
            if stage == 0:
                send(1, chunk)

            def earlier(half, carry):
                normed = normalize(landed[half, stage, rows(chunk)])
                pairs[:CHUNK] = jnp.dot(
                    normed, w_qkv[:, WIDTH:], preferred_element_type=jnp.float32
                ).astype(jnp.bfloat16)
                key_first = block_first(half) - GROUP * (stage + 1) + chunk * CHUNK
                key_marks = marks(key_first, CHUNK, 0.0, 1.0)
                for tile in range(CHUNKS):
                    if stage == 0 or tile <= chunk:
                        attend(
                            half,
                            tile,
                            pairs[:CHUNK, :WIDTH],
                            pairs[:CHUNK, WIDTH:],
                            key_marks,
                            False,
                            False,
                        )
                return carry

            lax.fori_loop(0, 2, earlier, 0)
            if stage == WIN - 1:
                if chunk == order[0]:
                    loads[2].wait()
                span = rows(chunk)
                for half in range(2):
                    mixed = []
                    for head in range(HEADS):
                        total = sums[half, span, wide_lanes(head)]
                        mixed.append((total[:, :128] / total[:, 128:]).astype(jnp.bfloat16))
                    result[half, span] = jnp.dot(
                        jnp.concatenate(mixed, axis=1), w_out[...], preferred_element_type=jnp.float32
                    ).astype(jnp.bfloat16)
                    pltpu.make_async_copy(
                        result.at[half, span], out.at[0, half, span], store_sem.at[half, chunk]
                    ).start()

    for chunk in order:
        for half in range(2):
            span = rows(chunk)
            pltpu.make_async_copy(
                result.at[half, span], out.at[0, half, span], store_sem.at[half, chunk]
            ).wait()
    for stage in range(WIN):
        for chunk in order:
            sent(stage, chunk)


def solution(mesh):
    count = mesh.shape["ctx"]

    def local(frames, episode_lengths, w_qkv, w_out):
        lengths = episode_lengths.reshape(1, -1)
        return pl.pallas_call(
            functools.partial(kernel, count),
            out_shape=jax.ShapeDtypeStruct(frames.shape, jnp.bfloat16),
            in_specs=[
                pl.BlockSpec(memory_space=pltpu.HBM),
                pl.BlockSpec(memory_space=pltpu.VMEM),
                pl.BlockSpec(memory_space=pltpu.HBM),
                pl.BlockSpec(memory_space=pltpu.HBM),
            ],
            out_specs=pl.BlockSpec(memory_space=pl.ANY),
            scratch_shapes=[
                pltpu.VMEM((2, GROUP, WIDTH), jnp.bfloat16),
                pltpu.VMEM((2, WIN, GROUP, WIDTH), jnp.bfloat16),
                pltpu.VMEM((WIDTH, 3 * WIDTH), jnp.bfloat16),
                pltpu.VMEM((WIDTH, WIDTH), jnp.bfloat16),
                pltpu.VMEM((2, GROUP, 2 * WIDTH), jnp.bfloat16),
                pltpu.VMEM((GROUP, 2 * WIDTH), jnp.bfloat16),
                pltpu.VMEM((2, GROUP, WIDTH), jnp.float32),
                pltpu.VMEM((2, GROUP, 2 * WIDTH), jnp.float32),
                pltpu.VMEM((2, GROUP, WIDTH), jnp.bfloat16),
                pltpu.VMEM((8, 128), jnp.float32),
                pltpu.SemaphoreType.DMA((3,)),
                pltpu.SemaphoreType.DMA((2, CHUNKS)),
                pltpu.SemaphoreType.DMA((2, WIN, CHUNKS)),
                pltpu.SemaphoreType.DMA((2, WIN, CHUNKS)),
            ],
            compiler_params=pltpu.CompilerParams(
                collective_id=0, has_side_effects=True, vmem_limit_bytes=48 * 1024 * 1024
            ),
        )(frames, lengths, w_qkv, w_out)

    in_specs = (P(("dp", "ctx"), None, None, None), P("dp"), P(), P())
    out_specs = P(("dp", "ctx"), None, None, None)
    return jax.shard_map(local, mesh=mesh, in_specs=in_specs, out_specs=out_specs, check_vma=False)
```

```python
import functools

import jax
import jax.numpy as jnp
from jax import lax
from jax.experimental import pallas as pl
from jax.experimental.pallas import tpu as pltpu
from jax.sharding import PartitionSpec as P

HEADS = 4
HEAD_DIM = 128
WIN = 2
GROUP = 512
WIDTH = 512
TILE = 256
ROWS = HEAD_DIM + 16
FAR = -(2.0**100)
RATE = HEAD_DIM ** (-0.5) * 1.4426950408889634
NEAR_PIECES = ((256, 256), (0, 256))
FAR_PIECES = ((256, 256), (128, 128), (0, 128))
MESH = pl.DeviceIdType.MESH
NT = (((1,), (1,)), ((), ()))


def normalize(rows):
    wide = rows.astype(jnp.float32)
    factor = lax.rsqrt(jnp.mean(wide * wide, axis=-1, keepdims=True) + 1e-06)
    return (wide * factor).astype(jnp.bfloat16)


def dot(a, b, dims=(((1,), (0,)), ((), ()))):
    return lax.dot_general(a, b, dims, preferred_element_type=jnp.float32)


def episode_bounds(lengths):
    count = lengths.shape[1]
    spread = jnp.broadcast_to(lengths.astype(jnp.float32), (128, count))
    row = lax.broadcasted_iota(jnp.int32, (128, count), 0)
    col = lax.broadcasted_iota(jnp.int32, (128, count), 1)
    column_ends = jnp.sum(jnp.where(col <= row, spread, 0.0), axis=1, keepdims=True)
    column_starts = jnp.sum(jnp.where(col < row, spread, 0.0), axis=1, keepdims=True)
    row = lax.broadcasted_iota(jnp.int32, (128, 128), 0)
    col = lax.broadcasted_iota(jnp.int32, (128, 128), 1)
    ends = jnp.sum(jnp.where(row == col, column_ends, 0.0), axis=0, keepdims=True)
    starts = jnp.sum(jnp.where(row == col, column_starts, 0.0), axis=0, keepdims=True)
    return starts, ends, column_starts, column_ends


def kernel(
    count,
    frames,
    lengths,
    w_qkv_hbm,
    w_out_hbm,
    out,
    own,
    landed,
    w_qkv,
    w_out,
    turned,
    queries,
    query_marks,
    peaks,
    sums,
    result,
    bounds,
    load_sem,
    store_sem,
    send_sem,
    recv_sem,
):
    place = lax.axis_index("ctx")
    right = lax.rem(place + 1, count)
    left = lax.rem(place + count - 1, count)
    first_place = place == 0
    last_place = place == count - 1

    barrier = pltpu.get_barrier_semaphore()
    for neighbour in (left, right):
        pl.semaphore_signal(barrier, inc=1, device_id={"ctx": neighbour}, device_id_type=MESH)

    loads = [
        pltpu.make_async_copy(frames.at[0], own, load_sem.at[0]),
        pltpu.make_async_copy(w_qkv_hbm, w_qkv, load_sem.at[1]),
        pltpu.make_async_copy(w_out_hbm, w_out, load_sem.at[2]),
    ]
    for load in loads:
        load.start()

    def pieces(stage):
        return NEAR_PIECES if stage == 0 else FAR_PIECES

    def rows(stage, piece):
        return pl.ds(*pieces(stage)[piece])

    def link(half, stage, piece):
        span = rows(stage, piece)
        source = frames.at[0, half, span] if stage == 0 else landed.at[half, 0, span]
        return pltpu.make_async_remote_copy(
            src_ref=source,
            dst_ref=landed.at[half, stage, span],
            send_sem=send_sem.at[half, stage, piece],
            recv_sem=recv_sem.at[half, stage, piece],
            device_id={"ctx": right if half == 0 else left},
            device_id_type=MESH,
        )

    def inside(stage, piece):
        span = rows(stage, piece)
        source = frames.at[0, 0, span] if stage == 0 else landed.at[0, 0, span]
        return pltpu.make_async_copy(
            source, landed.at[1, stage, span], recv_sem.at[1, stage, piece]
        )

    def send(stage, piece):
        link(0, stage, piece).start()

        @pl.when(jnp.logical_not(first_place))
        def _():
            link(1, stage, piece).start()

        @pl.when(last_place)
        def _():
            inside(stage, piece).start()

    def arrive(stage, piece):
        link(0, stage, piece).wait_recv()

        @pl.when(jnp.logical_not(last_place))
        def _():
            link(1, stage, piece).wait_recv()

        @pl.when(last_place)
        def _():
            inside(stage, piece).wait()

    def sent(stage, piece):
        link(0, stage, piece).wait_send()

        @pl.when(jnp.logical_not(first_place))
        def _():
            link(1, stage, piece).wait_send()

    def lanes(head):
        return slice(head * 128, head * 128 + 128)

    def block_first(half):
        return GROUP * (place + half * (2 * count - 1 - 2 * place))

    def key_marks(first, number):
        at = (first + lax.broadcasted_iota(jnp.int32, (number, 128), 0)).astype(jnp.float32)
        within = (at >= bounds[0:1, :]) & (at < bounds[1:2, :])
        return jnp.where(within, 0.0, 1.0).astype(jnp.bfloat16)

    def attend(half, first_query, number, keys, values, marks, diagonal, fresh):
        span = slice(first_query, first_query + number)
        keys_here = marks.shape[0]
        ones = jnp.ones((ROWS - HEAD_DIM, keys_here), jnp.bfloat16)
        if diagonal:
            key_at = lax.broadcasted_iota(jnp.int32, (keys_here, number), 0)
            query_at = first_query + lax.broadcasted_iota(jnp.int32, (keys_here, number), 1)
            behind = key_at <= query_at

        def score(head):
            key_part = jnp.concatenate([keys[:, lanes(head)], marks], axis=1)
            query_part = jnp.concatenate(
                [queries[half, lanes(head), span], query_marks[half, :, span]], axis=0
            )
            return dot(key_part, query_part)

        ahead = score(0)
        for head in range(HEADS):
            scores = ahead
            if head + 1 < HEADS:
                ahead = score(head + 1)
            if diagonal:
                scores = jnp.where(behind, scores, FAR)
            peak = jnp.max(scores, axis=0, keepdims=True)
            value_part = jnp.concatenate([values[lanes(head), :], ones], axis=0)
            if fresh:
                weights = jnp.exp2((scores - peak) * RATE).astype(jnp.bfloat16)
                sums[half, head, :, span] = dot(value_part, weights)
                peaks[half, head : head + 1, span] = peak
            else:
                before = peaks[half, head : head + 1, span]
                now = jnp.maximum(before, peak)
                scale = jnp.exp2((before - now) * RATE)
                weights = jnp.exp2((scores - now) * RATE).astype(jnp.bfloat16)
                sums[half, head, :, span] = sums[half, head, :, span] * scale + dot(
                    value_part, weights
                )
                peaks[half, head : head + 1, span] = now

    def project(normed):
        keys = dot(normed, w_qkv[:, WIDTH : 2 * WIDTH]).astype(jnp.bfloat16)
        values = dot(turned[WIDTH:, :], normed, NT).astype(jnp.bfloat16)
        return keys, values

    starts, ends, column_starts, column_ends = episode_bounds(lengths[...])
    bounds[0:1, :] = starts
    bounds[1:2, :] = ends

    pl.semaphore_wait(barrier, 2)
    send(0, 0)
    send(0, 1)

    loads[1].wait()
    turned[:WIDTH, :] = w_qkv[:, :WIDTH].T
    turned[WIDTH:, :] = w_qkv[:, 2 * WIDTH :].T
    loads[0].wait()

    def own_half(half, carry):
        base = block_first(half)
        at = (base + lax.broadcasted_iota(jnp.int32, (128, GROUP), 1)).astype(jnp.float32)
        within = (at >= column_starts) & (at < column_ends)
        query_marks[half] = jnp.where(within, FAR, 0.0).astype(jnp.bfloat16)
        normed = normalize(own[half])
        queries[half] = dot(turned[:WIDTH, :], normed, NT).astype(jnp.bfloat16)
        keys, values = project(normed)
        marks = key_marks(base, GROUP)
        for tile in range(GROUP // TILE):
            number = (tile + 1) * TILE
            attend(half, tile * TILE, TILE, keys[:number], values[:, :number], marks[:number], True, True)
        return carry

    lax.fori_loop(0, 2, own_half, 0)

    def earlier(stage, piece):
        low, number = pieces(stage)[piece]

        def body(half, carry):
            keys, values = project(normalize(landed[half, stage, low : low + number]))
            marks = key_marks(block_first(half) - GROUP * (stage + 1) + low, number)
            limit = GROUP if stage == 0 else low + number
            for first_query in range(0, limit, TILE):
                attend(
                    half, first_query, min(TILE, limit - first_query), keys, values, marks, False, False
                )
            return carry

        lax.fori_loop(0, 2, body, 0)

    def store(half, low, number):
        span = pl.ds(low, number)
        return pltpu.make_async_copy(
            result.at[half, span], out.at[0, half, span], store_sem.at[half, low // 128]
        )

    def finish(low, number):
        span = slice(low, low + number)
        for half in range(2):
            mixed = []
            for head in range(HEADS):
                inverse = 1.0 / sums[half, head, HEAD_DIM : HEAD_DIM + 1, span]
                mixed.append((sums[half, head, :HEAD_DIM, span] * inverse).astype(jnp.bfloat16))
            result[half, span] = dot(jnp.concatenate(mixed, axis=0).T, w_out[...]).astype(jnp.bfloat16)
            store(half, low, number).start()

    arrive(0, 0)
    send(1, 0)
    earlier(0, 0)
    arrive(0, 1)
    send(1, 1)
    send(1, 2)
    earlier(0, 1)
    loads[2].wait()
    for piece, (low, number) in enumerate(FAR_PIECES):
        arrive(1, piece)
        earlier(1, piece)
        finish(low, number)

    for low, number in FAR_PIECES:
        for half in range(2):
            store(half, low, number).wait()
    for stage in range(WIN):
        for piece in range(len(pieces(stage))):
            sent(stage, piece)


def solution(mesh):
    count = mesh.shape["ctx"]

    def local(frames, episode_lengths, w_qkv, w_out):
        lengths = episode_lengths.reshape(1, -1)
        return pl.pallas_call(
            functools.partial(kernel, count),
            out_shape=jax.ShapeDtypeStruct(frames.shape, jnp.bfloat16),
            in_specs=[
                pl.BlockSpec(memory_space=pltpu.HBM),
                pl.BlockSpec(memory_space=pltpu.VMEM),
                pl.BlockSpec(memory_space=pltpu.HBM),
                pl.BlockSpec(memory_space=pltpu.HBM),
            ],
            out_specs=pl.BlockSpec(memory_space=pl.ANY),
            scratch_shapes=[
                pltpu.VMEM((2, GROUP, WIDTH), jnp.bfloat16),
                pltpu.VMEM((2, WIN, GROUP, WIDTH), jnp.bfloat16),
                pltpu.VMEM((WIDTH, 3 * WIDTH), jnp.bfloat16),
                pltpu.VMEM((WIDTH, WIDTH), jnp.bfloat16),
                pltpu.VMEM((2 * WIDTH, WIDTH), jnp.bfloat16),
                pltpu.VMEM((2, WIDTH, GROUP), jnp.bfloat16),
                pltpu.VMEM((2, 128, GROUP), jnp.bfloat16),
                pltpu.VMEM((2, 8, GROUP), jnp.float32),
                pltpu.VMEM((2, HEADS, ROWS, GROUP), jnp.float32),
                pltpu.VMEM((2, GROUP, WIDTH), jnp.bfloat16),
                pltpu.VMEM((8, 128), jnp.float32),
                pltpu.SemaphoreType.DMA((3,)),
                pltpu.SemaphoreType.DMA((2, 4)),
                pltpu.SemaphoreType.DMA((2, WIN, 3)),
                pltpu.SemaphoreType.DMA((2, WIN, 3)),
            ],
            compiler_params=pltpu.CompilerParams(
                collective_id=0, has_side_effects=True, vmem_limit_bytes=62 * 1024 * 1024
            ),
        )(frames, lengths, w_qkv, w_out)

    in_specs = (P(("dp", "ctx"), None, None, None), P("dp"), P(), P())
    out_specs = P(("dp", "ctx"), None, None, None)
    return jax.shard_map(local, mesh=mesh, in_specs=in_specs, out_specs=out_specs, check_vma=False)
```

```python
import functools

import jax
import jax.numpy as jnp
from jax import lax
from jax.experimental import pallas as pl
from jax.experimental.pallas import tpu as pltpu
from jax.sharding import PartitionSpec as P

HEADS = 4
HEAD_DIM = 128
WIN = 2
GROUP = 512
WIDTH = 512
TILE = 256
ROWS = HEAD_DIM + 16
FAR = -(2.0**100)
RATE = HEAD_DIM ** (-0.5) * 1.4426950408889634
NEAR_PIECES = ((256, 256), (0, 256))
FAR_PIECES = ((256, 256), (128, 128), (0, 128))
MESH = pl.DeviceIdType.MESH
NT = (((1,), (1,)), ((), ()))


def normalize(rows):
    wide = rows.astype(jnp.float32)
    factor = lax.rsqrt(jnp.mean(wide * wide, axis=-1, keepdims=True) + 1e-06)
    return (wide * factor).astype(jnp.bfloat16)


def dot(a, b, dims=(((1,), (0,)), ((), ()))):
    return lax.dot_general(a, b, dims, preferred_element_type=jnp.float32)


def episode_bounds(lengths):
    count = lengths.shape[1]
    spread = jnp.broadcast_to(lengths.astype(jnp.float32), (128, count))
    row = lax.broadcasted_iota(jnp.int32, (128, count), 0)
    col = lax.broadcasted_iota(jnp.int32, (128, count), 1)
    column_ends = jnp.sum(jnp.where(col <= row, spread, 0.0), axis=1, keepdims=True)
    column_starts = jnp.sum(jnp.where(col < row, spread, 0.0), axis=1, keepdims=True)
    row = lax.broadcasted_iota(jnp.int32, (128, 128), 0)
    col = lax.broadcasted_iota(jnp.int32, (128, 128), 1)
    ends = jnp.sum(jnp.where(row == col, column_ends, 0.0), axis=0, keepdims=True)
    starts = jnp.sum(jnp.where(row == col, column_starts, 0.0), axis=0, keepdims=True)
    return starts, ends, column_starts, column_ends


def kernel(
    count,
    frames,
    lengths_hbm,
    w_qkv_hbm,
    w_out_hbm,
    out,
    own,
    landed,
    w_qkv,
    w_out,
    turned,
    queries,
    query_marks,
    peaks,
    sums,
    result,
    bounds,
    lengths,
    load_sem,
    store_sem,
    send_sem,
    recv_sem,
):
    place = lax.axis_index("ctx")
    right = lax.rem(place + 1, count)
    left = lax.rem(place + count - 1, count)
    first_place = place == 0
    last_place = place == count - 1

    barrier = pltpu.get_barrier_semaphore()
    for neighbour in (left, right):
        pl.semaphore_signal(barrier, inc=1, device_id={"ctx": neighbour}, device_id_type=MESH)

    loads = [
        pltpu.make_async_copy(frames.at[0], own, load_sem.at[0]),
        pltpu.make_async_copy(w_qkv_hbm, w_qkv, load_sem.at[1]),
        pltpu.make_async_copy(w_out_hbm, w_out, load_sem.at[2]),
        pltpu.make_async_copy(lengths_hbm, lengths, load_sem.at[3]),
    ]
    for load in loads:
        load.start()

    def pieces(stage):
        return NEAR_PIECES if stage == 0 else FAR_PIECES

    def rows(stage, piece):
        return pl.ds(*pieces(stage)[piece])

    def link(half, stage, piece):
        span = rows(stage, piece)
        source = frames.at[0, half, span] if stage == 0 else landed.at[half, 0, span]
        return pltpu.make_async_remote_copy(
            src_ref=source,
            dst_ref=landed.at[half, stage, span],
            send_sem=send_sem.at[half, stage, piece],
            recv_sem=recv_sem.at[half, stage, piece],
            device_id={"ctx": right if half == 0 else left},
            device_id_type=MESH,
        )

    def inside(stage, piece):
        span = rows(stage, piece)
        source = frames.at[0, 0, span] if stage == 0 else landed.at[0, 0, span]
        return pltpu.make_async_copy(
            source, landed.at[1, stage, span], recv_sem.at[1, stage, piece]
        )

    def send(stage, piece):
        link(0, stage, piece).start()

        @pl.when(jnp.logical_not(first_place))
        def _():
            link(1, stage, piece).start()

        @pl.when(last_place)
        def _():
            inside(stage, piece).start()

    def arrive(stage, piece):
        link(0, stage, piece).wait_recv()

        @pl.when(jnp.logical_not(last_place))
        def _():
            link(1, stage, piece).wait_recv()

        @pl.when(last_place)
        def _():
            inside(stage, piece).wait()

    def sent(stage, piece):
        link(0, stage, piece).wait_send()

        @pl.when(jnp.logical_not(first_place))
        def _():
            link(1, stage, piece).wait_send()

    def lanes(head):
        return slice(head * 128, head * 128 + 128)

    def block_first(half):
        return GROUP * (place + half * (2 * count - 1 - 2 * place))

    def key_marks(first, number):
        at = (first + lax.broadcasted_iota(jnp.int32, (number, 128), 0)).astype(jnp.float32)
        within = (at >= bounds[0:1, :]) & (at < bounds[1:2, :])
        return jnp.where(within, 0.0, 1.0).astype(jnp.bfloat16)

    def scores_of(half, head, first_query, number, keys, values, marks, diagonal):
        span = slice(first_query, first_query + number)
        key_part = jnp.concatenate([keys[:, lanes(head)], marks], axis=1)
        query_part = jnp.concatenate(
            [queries[half, lanes(head), span], query_marks[half, :, span]], axis=0
        )
        return dot(key_part, query_part)

    def weigh(scores, half, head, first_query, number, keys, values, marks, diagonal):
        span = slice(first_query, first_query + number)
        keys_here = marks.shape[0]
        if diagonal:
            key_at = lax.broadcasted_iota(jnp.int32, (keys_here, number), 0)
            query_at = first_query + lax.broadcasted_iota(jnp.int32, (keys_here, number), 1)
            scores = jnp.where(key_at <= query_at, scores, FAR)
        peak = jnp.max(scores, axis=0, keepdims=True)
        scale = None
        if not diagonal:
            before = peaks[half, head : head + 1, span]
            peak = jnp.maximum(before, peak)
            scale = jnp.exp2((before - peak) * RATE)
        peaks[half, head : head + 1, span] = peak
        return jnp.exp2((scores - peak) * RATE).astype(jnp.bfloat16), scale

    def mix(weights, scale, half, head, first_query, number, keys, values, marks, diagonal):
        span = slice(first_query, first_query + number)
        ones = jnp.ones((ROWS - HEAD_DIM, marks.shape[0]), jnp.bfloat16)
        value_part = jnp.concatenate([values[lanes(head), :], ones], axis=0)
        total = dot(value_part, weights)
        if not diagonal:
            total = sums[half, head, :, span] * scale + total
        sums[half, head, :, span] = total

    def attend(work):
        every = [scores_of(*item) for item in work]
        last = None
        for scores, item in zip(every, work):
            weights, scale = weigh(scores, *item)
            if last is not None:
                mix(*last)
            last = (weights, scale, *item)
        mix(*last)

    def project(normed):
        keys = dot(normed, w_qkv[:, WIDTH : 2 * WIDTH]).astype(jnp.bfloat16)
        values = dot(turned[WIDTH:, :], normed, NT).astype(jnp.bfloat16)
        return keys, values

    pl.semaphore_wait(barrier, 2)
    send(0, 0)
    send(0, 1)

    loads[3].wait()
    starts, ends, column_starts, column_ends = episode_bounds(lengths[...])
    bounds[0:1, :] = starts
    bounds[1:2, :] = ends
    loads[1].wait()
    turned[:WIDTH, :] = w_qkv[:, :WIDTH].T
    turned[WIDTH:, :] = w_qkv[:, 2 * WIDTH :].T
    loads[0].wait()

    def own_half(half, carry):
        base = block_first(half)
        at = (base + lax.broadcasted_iota(jnp.int32, (128, GROUP), 1)).astype(jnp.float32)
        within = (at >= column_starts) & (at < column_ends)
        query_marks[half] = jnp.where(within, FAR, 0.0).astype(jnp.bfloat16)
        normed = normalize(own[half])
        queries[half] = dot(turned[:WIDTH, :], normed, NT).astype(jnp.bfloat16)
        keys, values = project(normed)
        marks = key_marks(base, GROUP)
        work = []
        for first_query in range(0, GROUP, TILE):
            number = first_query + TILE
            for head in range(HEADS):
                work.append(
                    (half, head, first_query, TILE, keys[:number], values[:, :number], marks[:number], True)
                )
        attend(work)
        return carry

    lax.fori_loop(0, 2, own_half, 0)

    def earlier(stage, piece, together=False):
        low, number = pieces(stage)[piece]

        limit = GROUP if stage == 0 else low + number

        def prepare(half):
            keys, values = project(normalize(landed[half, stage, low : low + number]))
            marks = key_marks(block_first(half) - GROUP * (stage + 1) + low, number)
            return [(half, head, 0, limit, keys, values, marks, False) for head in range(HEADS)]

        def body(half, carry):
            attend(prepare(half))
            return carry

        if together:
            attend(prepare(0) + prepare(1))
        else:
            lax.fori_loop(0, 2, body, 0)

    def store(half, low, number):
        span = pl.ds(low, number)
        return pltpu.make_async_copy(
            result.at[half, span], out.at[0, half, span], store_sem.at[half, low // 128]
        )

    def finish(low, number):
        span = slice(low, low + number)
        for half in range(2):
            mixed = []
            for head in range(HEADS):
                inverse = 1.0 / sums[half, head, HEAD_DIM : HEAD_DIM + 1, span]
                mixed.append((sums[half, head, :HEAD_DIM, span] * inverse).astype(jnp.bfloat16))
            result[half, span] = dot(jnp.concatenate(mixed, axis=0).T, w_out[...]).astype(jnp.bfloat16)
            store(half, low, number).start()

    arrive(0, 0)
    send(1, 0)
    earlier(0, 0)
    arrive(0, 1)
    send(1, 1)
    send(1, 2)
    earlier(0, 1)
    loads[2].wait()
    for piece, (low, number) in enumerate(FAR_PIECES):
        arrive(1, piece)
        earlier(1, piece, piece > 0)
        finish(low, number)

    for low, number in FAR_PIECES:
        for half in range(2):
            store(half, low, number).wait()
    for stage in range(WIN):
        for piece in range(len(pieces(stage))):
            sent(stage, piece)


def solution(mesh):
    count = mesh.shape["ctx"]

    def local(frames, episode_lengths, w_qkv, w_out):
        lengths = episode_lengths.reshape(1, -1)
        return pl.pallas_call(
            functools.partial(kernel, count),
            out_shape=jax.ShapeDtypeStruct(frames.shape, jnp.bfloat16),
            in_specs=[
                pl.BlockSpec(memory_space=pltpu.HBM),
                pl.BlockSpec(memory_space=pltpu.HBM),
                pl.BlockSpec(memory_space=pltpu.HBM),
                pl.BlockSpec(memory_space=pltpu.HBM),
            ],
            out_specs=pl.BlockSpec(memory_space=pl.ANY),
            scratch_shapes=[
                pltpu.VMEM((2, GROUP, WIDTH), jnp.bfloat16),
                pltpu.VMEM((2, WIN, GROUP, WIDTH), jnp.bfloat16),
                pltpu.VMEM((WIDTH, 3 * WIDTH), jnp.bfloat16),
                pltpu.VMEM((WIDTH, WIDTH), jnp.bfloat16),
                pltpu.VMEM((2 * WIDTH, WIDTH), jnp.bfloat16),
                pltpu.VMEM((2, WIDTH, GROUP), jnp.bfloat16),
                pltpu.VMEM((2, 128, GROUP), jnp.bfloat16),
                pltpu.VMEM((2, 8, GROUP), jnp.float32),
                pltpu.VMEM((2, HEADS, ROWS, GROUP), jnp.float32),
                pltpu.VMEM((2, GROUP, WIDTH), jnp.bfloat16),
                pltpu.VMEM((8, 128), jnp.float32),
                pltpu.VMEM(lengths.shape, jnp.int32),
                pltpu.SemaphoreType.DMA((4,)),
                pltpu.SemaphoreType.DMA((2, 4)),
                pltpu.SemaphoreType.DMA((2, WIN, 3)),
                pltpu.SemaphoreType.DMA((2, WIN, 3)),
            ],
            compiler_params=pltpu.CompilerParams(
                collective_id=0, has_side_effects=True, vmem_limit_bytes=62 * 1024 * 1024
            ),
        )(frames, lengths, w_qkv, w_out)

    in_specs = (P(("dp", "ctx"), None, None, None), P("dp"), P(), P())
    out_specs = P(("dp", "ctx"), None, None, None)
    return jax.shard_map(local, mesh=mesh, in_specs=in_specs, out_specs=out_specs, check_vma=False)
```

```python
import functools

import jax
import jax.numpy as jnp
from jax import lax
from jax.experimental import pallas as pl
from jax.experimental.pallas import tpu as pltpu
from jax.sharding import PartitionSpec as P

HEADS = 4
HEAD_DIM = 128
WIN = 2
GROUP = 512
WIDTH = 512
TILE = 256
ROWS = HEAD_DIM + 16
FAR = -(2.0**100)
RATE = HEAD_DIM ** (-0.5) * 1.4426950408889634
NEAR_PIECES = ((256, 256), (0, 256))
FAR_PIECES = ((256, 256), (128, 128), (0, 128))
MESH = pl.DeviceIdType.MESH
NT = (((1,), (1,)), ((), ()))


def normalize(rows):
    wide = rows.astype(jnp.float32)
    factor = lax.rsqrt(jnp.mean(wide * wide, axis=-1, keepdims=True) + 1e-06)
    return (wide * factor).astype(jnp.bfloat16)


def dot(a, b, dims=(((1,), (0,)), ((), ()))):
    return lax.dot_general(a, b, dims, preferred_element_type=jnp.float32)


def episode_bounds(lengths):
    count = lengths.shape[1]
    spread = jnp.broadcast_to(lengths.astype(jnp.float32), (128, count))
    row = lax.broadcasted_iota(jnp.int32, (128, count), 0)
    col = lax.broadcasted_iota(jnp.int32, (128, count), 1)
    column_ends = jnp.sum(jnp.where(col <= row, spread, 0.0), axis=1, keepdims=True)
    column_starts = jnp.sum(jnp.where(col < row, spread, 0.0), axis=1, keepdims=True)
    row = lax.broadcasted_iota(jnp.int32, (128, 128), 0)
    col = lax.broadcasted_iota(jnp.int32, (128, 128), 1)
    ends = jnp.sum(jnp.where(row == col, column_ends, 0.0), axis=0, keepdims=True)
    starts = jnp.sum(jnp.where(row == col, column_starts, 0.0), axis=0, keepdims=True)
    return starts, ends, column_starts, column_ends


def kernel(
    count,
    frames,
    lengths_hbm,
    w_qkv_hbm,
    w_out_hbm,
    out,
    own,
    landed,
    w_qkv,
    w_out,
    turned,
    queries,
    query_marks,
    peaks,
    sums,
    bounds,
    lengths,
    load_sem,
    send_sem,
    recv_sem,
):
    place = lax.axis_index("ctx")
    right = lax.rem(place + 1, count)
    left = lax.rem(place + count - 1, count)
    first_place = place == 0
    last_place = place == count - 1

    barrier = pltpu.get_barrier_semaphore()
    for neighbour in (left, right):
        pl.semaphore_signal(barrier, inc=1, device_id={"ctx": neighbour}, device_id_type=MESH)

    loads = [
        pltpu.make_async_copy(frames.at[0], own, load_sem.at[0]),
        pltpu.make_async_copy(w_qkv_hbm, w_qkv, load_sem.at[1]),
        pltpu.make_async_copy(w_out_hbm, w_out, load_sem.at[2]),
        pltpu.make_async_copy(lengths_hbm, lengths, load_sem.at[3]),
    ]
    for load in loads:
        load.start()

    def pieces(stage):
        return NEAR_PIECES if stage == 0 else FAR_PIECES

    def rows(stage, piece):
        return pl.ds(*pieces(stage)[piece])

    def link(half, stage, piece):
        span = rows(stage, piece)
        source = frames.at[0, half, span] if stage == 0 else landed.at[half, 0, span]
        return pltpu.make_async_remote_copy(
            src_ref=source,
            dst_ref=landed.at[half, stage, span],
            send_sem=send_sem.at[half, stage, piece],
            recv_sem=recv_sem.at[half, stage, piece],
            device_id={"ctx": right if half == 0 else left},
            device_id_type=MESH,
        )

    def inside(stage, piece):
        span = rows(stage, piece)
        source = frames.at[0, 0, span] if stage == 0 else landed.at[0, 0, span]
        return pltpu.make_async_copy(
            source, landed.at[1, stage, span], recv_sem.at[1, stage, piece]
        )

    def send(stage, piece):
        link(0, stage, piece).start()

        @pl.when(jnp.logical_not(first_place))
        def _():
            link(1, stage, piece).start()

        @pl.when(last_place)
        def _():
            inside(stage, piece).start()

    def arrive(stage, piece):
        link(0, stage, piece).wait_recv()

        @pl.when(jnp.logical_not(last_place))
        def _():
            link(1, stage, piece).wait_recv()

        @pl.when(last_place)
        def _():
            inside(stage, piece).wait()

    def sent(stage, piece):
        link(0, stage, piece).wait_send()

        @pl.when(jnp.logical_not(first_place))
        def _():
            link(1, stage, piece).wait_send()

    def lanes(head):
        return slice(head * 128, head * 128 + 128)

    def block_first(half):
        return GROUP * (place + half * (2 * count - 1 - 2 * place))

    def key_marks(first, number):
        at = (first + lax.broadcasted_iota(jnp.int32, (number, 128), 0)).astype(jnp.float32)
        within = (at >= bounds[0:1, :]) & (at < bounds[1:2, :])
        return jnp.where(within, 0.0, 1.0).astype(jnp.bfloat16)

    def scores_of(half, head, first_query, number, keys, values, marks, diagonal):
        span = slice(first_query, first_query + number)
        key_part = jnp.concatenate([keys[:, lanes(head)], marks], axis=1)
        query_part = jnp.concatenate(
            [queries[half, lanes(head), span], query_marks[half, :, span]], axis=0
        )
        return dot(key_part, query_part)

    def weigh(scores, half, head, first_query, number, keys, values, marks, diagonal):
        span = slice(first_query, first_query + number)
        keys_here = marks.shape[0]
        if diagonal:
            key_at = lax.broadcasted_iota(jnp.int32, (keys_here, number), 0)
            query_at = first_query + lax.broadcasted_iota(jnp.int32, (keys_here, number), 1)
            scores = jnp.where(key_at <= query_at, scores, FAR)
        peak = jnp.max(scores, axis=0, keepdims=True)
        scale = None
        if not diagonal:
            before = peaks[half, head : head + 1, span]
            peak = jnp.maximum(before, peak)
            scale = jnp.exp2((before - peak) * RATE)
        peaks[half, head : head + 1, span] = peak
        return jnp.exp2((scores - peak) * RATE).astype(jnp.bfloat16), scale

    def mix(weights, scale, half, head, first_query, number, keys, values, marks, diagonal):
        span = slice(first_query, first_query + number)
        ones = jnp.ones((ROWS - HEAD_DIM, marks.shape[0]), jnp.bfloat16)
        value_part = jnp.concatenate([values[lanes(head), :], ones], axis=0)
        total = dot(value_part, weights)
        if not diagonal:
            total = sums[half, head, :, span] * scale + total
        sums[half, head, :, span] = total

    def attend(work):
        every = [scores_of(*item) for item in work]
        last = None
        for scores, item in zip(every, work):
            weights, scale = weigh(scores, *item)
            if last is not None:
                mix(*last)
            last = (weights, scale, *item)
        mix(*last)

    def project(normed):
        keys = dot(normed, w_qkv[:, WIDTH : 2 * WIDTH]).astype(jnp.bfloat16)
        values = dot(turned[WIDTH:, :], normed, NT).astype(jnp.bfloat16)
        return keys, values

    pl.semaphore_wait(barrier, 2)
    send(0, 0)
    send(0, 1)

    loads[3].wait()
    starts, ends, column_starts, column_ends = episode_bounds(lengths[...])
    bounds[0:1, :] = starts
    bounds[1:2, :] = ends
    loads[1].wait()
    turned[:WIDTH, :] = w_qkv[:, :WIDTH].T
    turned[WIDTH:, :] = w_qkv[:, 2 * WIDTH :].T
    loads[0].wait()

    def own_half(half, carry):
        base = block_first(half)
        at = (base + lax.broadcasted_iota(jnp.int32, (128, GROUP), 1)).astype(jnp.float32)
        within = (at >= column_starts) & (at < column_ends)
        query_marks[half] = jnp.where(within, FAR, 0.0).astype(jnp.bfloat16)
        normed = normalize(own[half])
        queries[half] = dot(turned[:WIDTH, :], normed, NT).astype(jnp.bfloat16)
        keys, values = project(normed)
        marks = key_marks(base, GROUP)
        work = []
        for first_query in range(0, GROUP, TILE):
            number = first_query + TILE
            for head in range(HEADS):
                work.append(
                    (half, head, first_query, TILE, keys[:number], values[:, :number], marks[:number], True)
                )
        attend(work)
        return carry

    lax.fori_loop(0, 2, own_half, 0)

    def earlier(stage, piece, together=False):
        low, number = pieces(stage)[piece]

        limit = GROUP if stage == 0 else low + number

        def prepare(half, keys, values):
            marks = key_marks(block_first(half) - GROUP * (stage + 1) + low, number)
            return [(half, head, 0, limit, keys, values, marks, False) for head in range(HEADS)]

        span = slice(low, low + number)
        if together:
            both = jnp.concatenate([landed[0, stage, span], landed[1, stage, span]], axis=0)
            keys, values = project(normalize(both))
            attend(
                prepare(0, keys[:number], values[:, :number])
                + prepare(1, keys[number:], values[:, number:])
            )
        else:

            def body(half, carry):
                attend(prepare(half, *project(normalize(landed[half, stage, span]))))
                return carry

            lax.fori_loop(0, 2, body, 0)

    def finish(low, number):
        span = slice(low, low + number)
        mixed = []
        for half in range(2):
            parts = []
            for head in range(HEADS):
                inverse = 1.0 / sums[half, head, HEAD_DIM : HEAD_DIM + 1, span]
                parts.append((sums[half, head, :HEAD_DIM, span] * inverse).astype(jnp.bfloat16))
            mixed.append(jnp.concatenate(parts, axis=0).T)
        result = dot(jnp.concatenate(mixed, axis=0), w_out[...]).astype(jnp.bfloat16)
        out[0, 0, span] = result[:number]
        out[0, 1, span] = result[number:]

    arrive(0, 0)
    send(1, 0)
    earlier(0, 0)
    arrive(0, 1)
    send(1, 1)
    send(1, 2)
    earlier(0, 1)
    loads[2].wait()
    for piece, (low, number) in enumerate(FAR_PIECES):
        arrive(1, piece)
        earlier(1, piece, piece > 0)
        finish(low, number)

    for stage in range(WIN):
        for piece in range(len(pieces(stage))):
            sent(stage, piece)


def solution(mesh):
    count = mesh.shape["ctx"]

    def local(frames, episode_lengths, w_qkv, w_out):
        lengths = episode_lengths.reshape(1, -1)
        return pl.pallas_call(
            functools.partial(kernel, count),
            out_shape=pltpu.VMEM(frames.shape, jnp.bfloat16),
            in_specs=[
                pl.BlockSpec(memory_space=pltpu.HBM),
                pl.BlockSpec(memory_space=pltpu.HBM),
                pl.BlockSpec(memory_space=pltpu.HBM),
                pl.BlockSpec(memory_space=pltpu.HBM),
            ],
            out_specs=pl.BlockSpec(memory_space=pltpu.VMEM),
            scratch_shapes=[
                pltpu.VMEM((2, GROUP, WIDTH), jnp.bfloat16),
                pltpu.VMEM((2, WIN, GROUP, WIDTH), jnp.bfloat16),
                pltpu.VMEM((WIDTH, 3 * WIDTH), jnp.bfloat16),
                pltpu.VMEM((WIDTH, WIDTH), jnp.bfloat16),
                pltpu.VMEM((2 * WIDTH, WIDTH), jnp.bfloat16),
                pltpu.VMEM((2, WIDTH, GROUP), jnp.bfloat16),
                pltpu.VMEM((2, 128, GROUP), jnp.bfloat16),
                pltpu.VMEM((2, 8, GROUP), jnp.float32),
                pltpu.VMEM((2, HEADS, ROWS, GROUP), jnp.float32),
                pltpu.VMEM((8, 128), jnp.float32),
                pltpu.VMEM(lengths.shape, jnp.int32),
                pltpu.SemaphoreType.DMA((4,)),
                pltpu.SemaphoreType.DMA((2, WIN, 3)),
                pltpu.SemaphoreType.DMA((2, WIN, 3)),
            ],
            compiler_params=pltpu.CompilerParams(
                collective_id=0, has_side_effects=True, vmem_limit_bytes=58 * 1024 * 1024
            ),
        )(frames, lengths, w_qkv, w_out)

    in_specs = (P(("dp", "ctx"), None, None, None), P("dp"), P(), P())
    out_specs = P(("dp", "ctx"), None, None, None)
    return jax.shard_map(local, mesh=mesh, in_specs=in_specs, out_specs=out_specs, check_vma=False)
```

```python
import functools

import jax
import jax.numpy as jnp
from jax import lax
from jax.experimental import pallas as pl
from jax.experimental.pallas import tpu as pltpu
from jax.sharding import PartitionSpec as P

HEADS = 4
HEAD_DIM = 128
WIN = 2
GROUP = 512
WIDTH = 512
TILE = 256
ROWS = HEAD_DIM + 16
FAR = -(2.0**100)
RATE = HEAD_DIM ** (-0.5) * 1.4426950408889634
NEAR_PIECES = ((256, 256), (0, 256))
FAR_PIECES = ((256, 256), (128, 128), (0, 128))
MESH = pl.DeviceIdType.MESH
NT = (((1,), (1,)), ((), ()))


def normalize(rows):
    wide = rows.astype(jnp.float32)
    factor = lax.rsqrt(jnp.mean(wide * wide, axis=-1, keepdims=True) + 1e-06)
    return (wide * factor).astype(jnp.bfloat16)


def dot(a, b, dims=(((1,), (0,)), ((), ()))):
    return lax.dot_general(a, b, dims, preferred_element_type=jnp.float32)


def episode_bounds(lengths):
    count = lengths.shape[1]
    spread = jnp.broadcast_to(lengths.astype(jnp.float32), (128, count))
    row = lax.broadcasted_iota(jnp.int32, (128, count), 0)
    col = lax.broadcasted_iota(jnp.int32, (128, count), 1)
    column_ends = jnp.sum(jnp.where(col <= row, spread, 0.0), axis=1, keepdims=True)
    column_starts = jnp.sum(jnp.where(col < row, spread, 0.0), axis=1, keepdims=True)
    row = lax.broadcasted_iota(jnp.int32, (128, 128), 0)
    col = lax.broadcasted_iota(jnp.int32, (128, 128), 1)
    ends = jnp.sum(jnp.where(row == col, column_ends, 0.0), axis=0, keepdims=True)
    starts = jnp.sum(jnp.where(row == col, column_starts, 0.0), axis=0, keepdims=True)
    return starts, ends, column_starts, column_ends


def kernel(
    count,
    frames,
    lengths_hbm,
    w_qkv_hbm,
    w_out_hbm,
    out,
    waiting,
    w_out,
    own,
    landed,
    w_qkv,
    turned,
    queries,
    query_marks,
    peaks,
    sums,
    bounds,
    folded,
    barred,
    lengths,
    load_sem,
    send_sem,
    recv_sem,
):
    place = lax.axis_index("ctx")
    right = lax.rem(place + 1, count)
    left = lax.rem(place + count - 1, count)
    first_place = place == 0
    last_place = place == count - 1

    barrier = pltpu.get_barrier_semaphore()
    for neighbour in (left, right):
        pl.semaphore_signal(barrier, inc=1, device_id={"ctx": neighbour}, device_id_type=MESH)

    loads = [
        pltpu.make_async_copy(frames.at[0], own, load_sem.at[0]),
        pltpu.make_async_copy(w_qkv_hbm, w_qkv, load_sem.at[1]),
        pltpu.make_async_copy(w_out_hbm, w_out, load_sem.at[2]),
        pltpu.make_async_copy(lengths_hbm, lengths, load_sem.at[3]),
    ]
    for load in loads:
        load.start()

    def pieces(stage):
        return NEAR_PIECES if stage == 0 else FAR_PIECES

    def rows(stage, piece):
        return pl.ds(*pieces(stage)[piece])

    def link(half, stage, piece):
        span = rows(stage, piece)
        source = frames.at[0, half, span] if stage == 0 else landed.at[half, 0, span]
        return pltpu.make_async_remote_copy(
            src_ref=source,
            dst_ref=landed.at[half, stage, span],
            send_sem=send_sem.at[half, stage, piece],
            recv_sem=recv_sem.at[half, stage, piece],
            device_id={"ctx": right if half == 0 else left},
            device_id_type=MESH,
        )

    def inside(stage, piece):
        span = rows(stage, piece)
        source = frames.at[0, 0, span] if stage == 0 else landed.at[0, 0, span]
        return pltpu.make_async_copy(
            source, landed.at[1, stage, span], recv_sem.at[1, stage, piece]
        )

    def send(stage, piece):
        link(0, stage, piece).start()

        @pl.when(jnp.logical_not(first_place))
        def _():
            link(1, stage, piece).start()

        @pl.when(last_place)
        def _():
            inside(stage, piece).start()

    def arrive(stage, piece):
        link(0, stage, piece).wait_recv()

        @pl.when(jnp.logical_not(last_place))
        def _():
            link(1, stage, piece).wait_recv()

        @pl.when(last_place)
        def _():
            inside(stage, piece).wait()

    def sent(stage, piece):
        link(0, stage, piece).wait_send()

        @pl.when(jnp.logical_not(first_place))
        def _():
            link(1, stage, piece).wait_send()

    def lanes(head):
        return slice(head * 128, head * 128 + 128)

    def block_first(half):
        return GROUP * (place + half * (2 * count - 1 - 2 * place))

    def key_marks(first, number):
        at = (first + lax.broadcasted_iota(jnp.int32, (number, 128), 0)).astype(jnp.float32)
        within = (at >= bounds[0:1, :]) & (at < bounds[1:2, :])
        return jnp.where(within, 0.0, 1.0).astype(jnp.bfloat16)

    def scores_of(half, head, first_query, number, keys, values, marks, diagonal):
        span = slice(first_query, first_query + number)
        key_part = jnp.concatenate([keys[:, lanes(head)], marks], axis=1)
        query_part = jnp.concatenate(
            [queries[half, lanes(head), span], query_marks[half, :, span]], axis=0
        )
        return dot(key_part, query_part)

    def weigh(scores, half, head, first_query, number, keys, values, marks, diagonal):
        span = slice(first_query, first_query + number)
        keys_here = marks.shape[0]
        if diagonal:
            key_at = lax.broadcasted_iota(jnp.int32, (keys_here, number), 0)
            query_at = first_query + lax.broadcasted_iota(jnp.int32, (keys_here, number), 1)
            scores = jnp.where(key_at <= query_at, scores, FAR)
        peak = jnp.max(scores, axis=0, keepdims=True)
        scale = None
        if not diagonal:
            before = peaks[half, head : head + 1, span]
            peak = jnp.maximum(before, peak)
            scale = jnp.exp2((before - peak) * RATE)
        peaks[half, head : head + 1, span] = peak
        return jnp.exp2((scores - peak) * RATE).astype(jnp.bfloat16), scale

    def mix(weights, scale, half, head, first_query, number, keys, values, marks, diagonal):
        span = slice(first_query, first_query + number)
        ones = jnp.ones((ROWS - HEAD_DIM, marks.shape[0]), jnp.bfloat16)
        value_part = jnp.concatenate([values[lanes(head), :], ones], axis=0)
        total = dot(value_part, weights)
        if not diagonal:
            total = sums[half, head, :, span] * scale + total
        sums[half, head, :, span] = total

    def attend(work):
        every = [scores_of(*item) for item in work]
        last = None
        for scores, item in zip(every, work):
            weights, scale = weigh(scores, *item)
            if last is not None:
                mix(*last)
            last = (weights, scale, *item)
        mix(*last)

    def project(normed):
        keys = dot(normed, w_qkv[:, WIDTH : 2 * WIDTH]).astype(jnp.bfloat16)
        values = dot(turned[WIDTH:, :], normed, NT).astype(jnp.bfloat16)
        return keys, values

    pl.semaphore_wait(barrier, 2)
    send(0, 0)
    send(0, 1)

    loads[3].wait()
    starts, ends, column_starts, column_ends = episode_bounds(lengths[...])
    bounds[0:1, :] = starts
    bounds[1:2, :] = ends
    loads[1].wait()
    turned[:WIDTH, :] = w_qkv[:, :WIDTH].T
    turned[WIDTH:, :] = w_qkv[:, 2 * WIDTH :].T
    loads[0].wait()

    def own_half(half, carry):
        base = block_first(half)
        at = (base + lax.broadcasted_iota(jnp.int32, (128, GROUP), 1)).astype(jnp.float32)
        within = (at >= column_starts) & (at < column_ends)
        query_marks[half] = jnp.where(within, FAR, 0.0).astype(jnp.bfloat16)
        normed = normalize(own[half])
        queries[half] = dot(turned[:WIDTH, :], normed, NT).astype(jnp.bfloat16)
        keys, values = project(normed)
        marks = key_marks(base, GROUP)
        work = []
        for first_query in range(0, GROUP, TILE):
            number = first_query + TILE
            for head in range(HEADS):
                work.append(
                    (half, head, first_query, TILE, keys[:number], values[:, :number], marks[:number], True)
                )
        attend(work)
        return carry

    lax.fori_loop(0, 2, own_half, 0)

    def earlier(stage, piece, together=False):
        low, number = pieces(stage)[piece]

        limit = GROUP if stage == 0 else low + number

        def prepare(half, keys, values):
            marks = key_marks(block_first(half) - GROUP * (stage + 1) + low, number)
            return [(half, head, 0, limit, keys, values, marks, False) for head in range(HEADS)]

        span = slice(low, low + number)
        if together:
            both = jnp.concatenate([landed[0, stage, span], landed[1, stage, span]], axis=0)
            keys, values = project(normalize(both))
            attend(
                prepare(0, keys[:number], values[:, :number])
                + prepare(1, keys[number:], values[:, number:])
            )
        else:

            def body(half, carry):
                attend(prepare(half, *project(normalize(landed[half, stage, span]))))
                return carry

            lax.fori_loop(0, 2, body, 0)

    def fold(half, carry):
        marks = key_marks(block_first(half) - GROUP * WIN, 128)
        barred[half] = dot(marks, query_marks[half, :, :128])
        for head in range(HEADS):
            key_weights = w_qkv[:, WIDTH + head * 128 : WIDTH + head * 128 + 128]
            folded[half, :, lanes(head)] = dot(key_weights, queries[half, lanes(head), :128]).astype(
                jnp.bfloat16
            )
        return carry

    def last():
        both = jnp.concatenate([landed[0, 1, :128], landed[1, 1, :128]], axis=0)
        normed = normalize(both)
        every = []
        for half in range(2):
            scores = dot(normed[half * 128 : half * 128 + 128], folded[half])
            every += [scores[:, lanes(head)] + barred[half] for head in range(HEADS)]
        values = dot(turned[WIDTH:, :], normed, NT).astype(jnp.bfloat16)
        marks = jnp.zeros((128, 128), jnp.bfloat16)
        ones = jnp.ones((ROWS - HEAD_DIM, 128), jnp.bfloat16)
        for half in range(2):
            for head in range(0, HEADS, 2):
                weights, scales, parts = [], [], []
                for one in (head, head + 1):
                    found = weigh(every[half * HEADS + one], half, one, 0, 128, None, None, marks, False)
                    weights.append(found[0])
                    scales.append(found[1])
                    part = values[lanes(one), half * 128 : half * 128 + 128]
                    parts.append(jnp.concatenate([part, ones], axis=0))
                blocks = jnp.concatenate(
                    [
                        jnp.concatenate([weights[0], marks], axis=1),
                        jnp.concatenate([marks, weights[1]], axis=1),
                    ],
                    axis=0,
                )
                total = dot(jnp.concatenate(parts, axis=1), blocks)
                for one in range(2):
                    sums[half, head + one, :, :128] = (
                        sums[half, head + one, :, :128] * scales[one] + total[:, lanes(one)]
                    )

    def finish(low, number):
        span = slice(low, low + number)
        mixed = []
        for half in range(2):
            parts = []
            for head in range(HEADS):
                inverse = 1.0 / sums[half, head, HEAD_DIM : HEAD_DIM + 1, span]
                parts.append((sums[half, head, :HEAD_DIM, span] * inverse).astype(jnp.bfloat16))
            mixed.append(jnp.concatenate(parts, axis=0).T)
        if low == 0:
            waiting[...] = jnp.concatenate(mixed, axis=0)
            return
        result = dot(jnp.concatenate(mixed, axis=0), w_out[...]).astype(jnp.bfloat16)
        done = slice(low - 128, low - 128 + number)
        out[0, done] = result[:number]
        out[1, done] = result[number:]

    arrive(0, 0)
    send(1, 0)
    earlier(0, 0)
    arrive(0, 1)
    send(1, 1)
    send(1, 2)
    earlier(0, 1)
    lax.fori_loop(0, 2, fold, 0)
    loads[2].wait()
    for piece, (low, number) in enumerate(FAR_PIECES):
        arrive(1, piece)
        if low > 0:
            earlier(1, piece, piece > 0)
        else:
            last()
        finish(low, number)

    for stage in range(WIN):
        for piece in range(len(pieces(stage))):
            sent(stage, piece)


def unload(done, waiting, w_out, out, result, sem):
    copies = [
        pltpu.make_async_copy(done.at[half], out.at[0, half, pl.ds(128, GROUP - 128)], sem.at[half])
        for half in range(2)
    ]
    for copy in copies:
        copy.start()
    result[...] = dot(waiting[...], w_out[...]).astype(jnp.bfloat16)
    lasts = [
        pltpu.make_async_copy(
            result.at[pl.ds(half * 128, 128)], out.at[0, half, pl.ds(0, 128)], sem.at[2 + half]
        )
        for half in range(2)
    ]
    for copy in lasts:
        copy.start()
    for copy in copies + lasts:
        copy.wait()


def solution(mesh):
    count = mesh.shape["ctx"]

    def local(frames, episode_lengths, w_qkv, w_out):
        lengths = episode_lengths.reshape(1, -1)
        parts = pl.pallas_call(
            functools.partial(kernel, count),
            out_shape=(
                pltpu.VMEM((2, GROUP - 128, WIDTH), jnp.bfloat16),
                pltpu.VMEM((256, WIDTH), jnp.bfloat16),
                pltpu.VMEM((WIDTH, WIDTH), jnp.bfloat16),
            ),
            in_specs=[
                pl.BlockSpec(memory_space=pltpu.HBM),
                pl.BlockSpec(memory_space=pltpu.HBM),
                pl.BlockSpec(memory_space=pltpu.HBM),
                pl.BlockSpec(memory_space=pltpu.HBM),
            ],
            out_specs=[pl.BlockSpec(memory_space=pltpu.VMEM)] * 3,
            scratch_shapes=[
                pltpu.VMEM((2, GROUP, WIDTH), jnp.bfloat16),
                pltpu.VMEM((2, WIN, GROUP, WIDTH), jnp.bfloat16),
                pltpu.VMEM((WIDTH, 3 * WIDTH), jnp.bfloat16),
                pltpu.VMEM((2 * WIDTH, WIDTH), jnp.bfloat16),
                pltpu.VMEM((2, WIDTH, GROUP), jnp.bfloat16),
                pltpu.VMEM((2, 128, GROUP), jnp.bfloat16),
                pltpu.VMEM((2, 8, GROUP), jnp.float32),
                pltpu.VMEM((2, HEADS, ROWS, GROUP), jnp.float32),
                pltpu.VMEM((8, 128), jnp.float32),
                pltpu.VMEM((2, WIDTH, WIDTH), jnp.bfloat16),
                pltpu.VMEM((2, 128, 128), jnp.float32),
                pltpu.VMEM(lengths.shape, jnp.int32),
                pltpu.SemaphoreType.DMA((4,)),
                pltpu.SemaphoreType.DMA((2, WIN, 3)),
                pltpu.SemaphoreType.DMA((2, WIN, 3)),
            ],
            compiler_params=pltpu.CompilerParams(
                collective_id=0, has_side_effects=True, vmem_limit_bytes=56 * 1024 * 1024
            ),
        )(frames, lengths, w_qkv, w_out)
        return pl.pallas_call(
            unload,
            out_shape=jax.ShapeDtypeStruct(frames.shape, jnp.bfloat16),
            in_specs=[pl.BlockSpec(memory_space=pltpu.VMEM)] * 3,
            out_specs=pl.BlockSpec(memory_space=pltpu.HBM),
            scratch_shapes=[
                pltpu.VMEM((256, WIDTH), jnp.bfloat16),
                pltpu.SemaphoreType.DMA((4,)),
            ],
            compiler_params=pltpu.CompilerParams(vmem_limit_bytes=4 * 1024 * 1024),
        )(*parts)

    in_specs = (P(("dp", "ctx"), None, None, None), P("dp"), P(), P())
    out_specs = P(("dp", "ctx"), None, None, None)
    return jax.shard_map(local, mesh=mesh, in_specs=in_specs, out_specs=out_specs, check_vma=False)
```

```python
import functools

import jax
import jax.numpy as jnp
from jax import lax
from jax.experimental import pallas as pl
from jax.experimental.pallas import tpu as pltpu
from jax.sharding import PartitionSpec as P

HEADS = 4
HEAD_DIM = 128
WIN = 2
GROUP = 512
WIDTH = 512
TILE = 256
ROWS = HEAD_DIM + 16
FAR = -(2.0**100)
RATE = HEAD_DIM ** (-0.5) * 1.4426950408889634
NEAR_PIECES = ((256, 256), (0, 256))
FAR_PIECES = ((256, 256), (128, 128), (0, 128))
MESH = pl.DeviceIdType.MESH
NT = (((1,), (1,)), ((), ()))


def normalize(rows):
    wide = rows.astype(jnp.float32)
    factor = lax.rsqrt(jnp.mean(wide * wide, axis=-1, keepdims=True) + 1e-06)
    return (wide * factor).astype(jnp.bfloat16)


def dot(a, b, dims=(((1,), (0,)), ((), ()))):
    return lax.dot_general(a, b, dims, preferred_element_type=jnp.float32)


def episode_bounds(lengths):
    count = lengths.shape[1]
    spread = jnp.broadcast_to(lengths.astype(jnp.float32), (128, count))
    row = lax.broadcasted_iota(jnp.int32, (128, count), 0)
    col = lax.broadcasted_iota(jnp.int32, (128, count), 1)
    column_ends = jnp.sum(jnp.where(col <= row, spread, 0.0), axis=1, keepdims=True)
    column_starts = jnp.sum(jnp.where(col < row, spread, 0.0), axis=1, keepdims=True)
    row = lax.broadcasted_iota(jnp.int32, (128, 128), 0)
    col = lax.broadcasted_iota(jnp.int32, (128, 128), 1)
    ends = jnp.sum(jnp.where(row == col, column_ends, 0.0), axis=0, keepdims=True)
    starts = jnp.sum(jnp.where(row == col, column_starts, 0.0), axis=0, keepdims=True)
    return starts, ends, column_starts, column_ends


def kernel(
    count,
    frames,
    lengths_hbm,
    w_qkv_hbm,
    w_out_hbm,
    out,
    waiting,
    w_out,
    own,
    landed,
    w_qkv,
    turned,
    queries,
    query_marks,
    peaks,
    sums,
    bounds,
    folded,
    barred,
    lengths,
    load_sem,
    send_sem,
    recv_sem,
):
    place = lax.axis_index("ctx")
    right = lax.rem(place + 1, count)
    left = lax.rem(place + count - 1, count)
    first_place = place == 0
    last_place = place == count - 1

    barrier = pltpu.get_barrier_semaphore()
    for neighbour in (left, right):
        pl.semaphore_signal(barrier, inc=1, device_id={"ctx": neighbour}, device_id_type=MESH)

    loads = [
        pltpu.make_async_copy(frames.at[0], own, load_sem.at[0]),
        pltpu.make_async_copy(w_qkv_hbm, w_qkv, load_sem.at[1]),
        pltpu.make_async_copy(w_out_hbm, w_out, load_sem.at[2]),
        pltpu.make_async_copy(lengths_hbm, lengths, load_sem.at[3]),
    ]
    for load in loads:
        load.start()

    def pieces(stage):
        return NEAR_PIECES if stage == 0 else FAR_PIECES

    def rows(stage, piece):
        return pl.ds(*pieces(stage)[piece])

    def link(half, stage, piece):
        span = rows(stage, piece)
        source = frames.at[0, half, span] if stage == 0 else landed.at[half, 0, span]
        return pltpu.make_async_remote_copy(
            src_ref=source,
            dst_ref=landed.at[half, stage, span],
            send_sem=send_sem.at[half, stage, piece],
            recv_sem=recv_sem.at[half, stage, piece],
            device_id={"ctx": right if half == 0 else left},
            device_id_type=MESH,
        )

    def inside(stage, piece):
        span = rows(stage, piece)
        source = frames.at[0, 0, span] if stage == 0 else landed.at[0, 0, span]
        return pltpu.make_async_copy(
            source, landed.at[1, stage, span], recv_sem.at[1, stage, piece]
        )

    def send(stage, piece):
        link(0, stage, piece).start()

        @pl.when(jnp.logical_not(first_place))
        def _():
            link(1, stage, piece).start()

        @pl.when(last_place)
        def _():
            inside(stage, piece).start()

    def arrive(stage, piece):
        link(0, stage, piece).wait_recv()

        @pl.when(jnp.logical_not(last_place))
        def _():
            link(1, stage, piece).wait_recv()

        @pl.when(last_place)
        def _():
            inside(stage, piece).wait()

    def sent(stage, piece):
        link(0, stage, piece).wait_send()

        @pl.when(jnp.logical_not(first_place))
        def _():
            link(1, stage, piece).wait_send()

    def lanes(head):
        return slice(head * 128, head * 128 + 128)

    def block_first(half):
        return GROUP * (place + half * (2 * count - 1 - 2 * place))

    def key_marks(first, number):
        at = (first + lax.broadcasted_iota(jnp.int32, (number, 128), 0)).astype(jnp.float32)
        within = (at >= bounds[0:1, :]) & (at < bounds[1:2, :])
        return jnp.where(within, 0.0, 1.0).astype(jnp.bfloat16)

    def scores_of(half, head, first_query, number, keys, values, marks, diagonal):
        span = slice(first_query, first_query + number)
        key_part = jnp.concatenate([keys[:, lanes(head)], marks], axis=1)
        query_part = jnp.concatenate(
            [queries[half, lanes(head), span], query_marks[half, :, span]], axis=0
        )
        return dot(key_part, query_part)

    def weigh(scores, half, head, first_query, number, keys, values, marks, diagonal):
        span = slice(first_query, first_query + number)
        keys_here = marks.shape[0]
        if diagonal:
            key_at = lax.broadcasted_iota(jnp.int32, (keys_here, number), 0)
            query_at = first_query + lax.broadcasted_iota(jnp.int32, (keys_here, number), 1)
            scores = jnp.where(key_at <= query_at, scores, FAR)
        peak = jnp.max(scores, axis=0, keepdims=True)
        scale = None
        if not diagonal:
            before = peaks[half, head : head + 1, span]
            peak = jnp.maximum(before, peak)
            scale = jnp.exp2((before - peak) * RATE)
        peaks[half, head : head + 1, span] = peak
        return jnp.exp2((scores - peak) * RATE).astype(jnp.bfloat16), scale

    def mix(weights, scale, half, head, first_query, number, keys, values, marks, diagonal):
        span = slice(first_query, first_query + number)
        ones = jnp.ones((ROWS - HEAD_DIM, marks.shape[0]), jnp.bfloat16)
        value_part = jnp.concatenate([values[lanes(head), :], ones], axis=0)
        total = dot(value_part, weights)
        if not diagonal:
            total = sums[half, head, :, span] * scale + total
        sums[half, head, :, span] = total

    def attend(work):
        every = [scores_of(*item) for item in work]
        last = None
        for scores, item in zip(every, work):
            weights, scale = weigh(scores, *item)
            if last is not None:
                mix(*last)
            last = (weights, scale, *item)
        mix(*last)

    def project(normed):
        keys = dot(normed, w_qkv[:, WIDTH : 2 * WIDTH]).astype(jnp.bfloat16)
        values = dot(turned[WIDTH:, :], normed, NT).astype(jnp.bfloat16)
        return keys, values

    pl.semaphore_wait(barrier, 2)
    send(0, 0)
    send(0, 1)

    loads[3].wait()
    starts, ends, column_starts, column_ends = episode_bounds(lengths[...])
    bounds[0:1, :] = starts
    bounds[1:2, :] = ends
    loads[1].wait()
    turned[:WIDTH, :] = w_qkv[:, :WIDTH].T
    turned[WIDTH:, :] = w_qkv[:, 2 * WIDTH :].T
    loads[0].wait()

    def own_half(half, carry):
        base = block_first(half)
        at = (base + lax.broadcasted_iota(jnp.int32, (128, GROUP), 1)).astype(jnp.float32)
        within = (at >= column_starts) & (at < column_ends)
        query_marks[half] = jnp.where(within, FAR, 0.0).astype(jnp.bfloat16)
        normed = normalize(own[half])
        queries[half] = dot(turned[:WIDTH, :], normed, NT).astype(jnp.bfloat16)
        keys, values = project(normed)
        marks = key_marks(base, GROUP)
        work = []
        for first_query in range(0, GROUP, TILE):
            number = first_query + TILE
            for head in range(HEADS):
                work.append(
                    (half, head, first_query, TILE, keys[:number], values[:, :number], marks[:number], True)
                )
        attend(work)
        return carry

    lax.fori_loop(0, 2, own_half, 0)

    def earlier(stage, piece, together=False):
        low, number = pieces(stage)[piece]

        limit = GROUP if stage == 0 else low + number

        def prepare(half, keys, values):
            marks = key_marks(block_first(half) - GROUP * (stage + 1) + low, number)
            return [(half, head, 0, limit, keys, values, marks, False) for head in range(HEADS)]

        span = slice(low, low + number)
        if together:
            both = jnp.concatenate([landed[0, stage, span], landed[1, stage, span]], axis=0)
            keys, values = project(normalize(both))
            attend(
                prepare(0, keys[:number], values[:, :number])
                + prepare(1, keys[number:], values[:, number:])
            )
        else:

            def body(half, carry):
                attend(prepare(half, *project(normalize(landed[half, stage, span]))))
                return carry

            lax.fori_loop(0, 2, body, 0)

    def fold(half, carry):
        marks = key_marks(block_first(half) - GROUP * WIN, 128)
        barred[half] = dot(marks, query_marks[half, :, :128])
        for head in range(HEADS):
            key_weights = w_qkv[:, WIDTH + head * 128 : WIDTH + head * 128 + 128]
            folded[half, :, lanes(head)] = dot(key_weights, queries[half, lanes(head), :128]).astype(
                jnp.bfloat16
            )
        return carry

    def last():
        both = jnp.concatenate([landed[0, 1, :128], landed[1, 1, :128]], axis=0)
        normed = normalize(both)
        every = []
        for half in range(2):
            scores = dot(normed[half * 128 : half * 128 + 128], folded[half])
            every += [scores[:, lanes(head)] + barred[half] for head in range(HEADS)]
        values = dot(turned[WIDTH:, :], normed, NT).astype(jnp.bfloat16)
        marks = jnp.zeros((128, 128), jnp.bfloat16)
        ones = jnp.ones((ROWS - HEAD_DIM, 128), jnp.bfloat16)
        for half in range(2):
            for head in range(0, HEADS, 2):
                weights, scales, parts = [], [], []
                for one in (head, head + 1):
                    found = weigh(every[half * HEADS + one], half, one, 0, 128, None, None, marks, False)
                    weights.append(found[0])
                    scales.append(found[1])
                    part = values[lanes(one), half * 128 : half * 128 + 128]
                    parts.append(jnp.concatenate([part, ones], axis=0))
                blocks = jnp.concatenate(
                    [
                        jnp.concatenate([weights[0], marks], axis=1),
                        jnp.concatenate([marks, weights[1]], axis=1),
                    ],
                    axis=0,
                )
                total = dot(jnp.concatenate(parts, axis=1), blocks)
                for one in range(2):
                    whole = sums[half, head + one, :, :128] * scales[one] + total[:, lanes(one)]
                    inverse = 1.0 / whole[HEAD_DIM : HEAD_DIM + 1]
                    done = (whole[:HEAD_DIM] * inverse).astype(jnp.bfloat16)
                    waiting[half * 128 : half * 128 + 128, lanes(head + one)] = done.T

    def finish(low, number):
        span = slice(low, low + number)
        mixed = []
        for half in range(2):
            parts = []
            for head in range(HEADS):
                inverse = 1.0 / sums[half, head, HEAD_DIM : HEAD_DIM + 1, span]
                parts.append((sums[half, head, :HEAD_DIM, span] * inverse).astype(jnp.bfloat16))
            mixed.append(jnp.concatenate(parts, axis=0).T)
        result = dot(jnp.concatenate(mixed, axis=0), w_out[...]).astype(jnp.bfloat16)
        done = slice(low - 128, low - 128 + number)
        out[0, done] = result[:number]
        out[1, done] = result[number:]

    arrive(0, 0)
    send(1, 0)
    earlier(0, 0)
    arrive(0, 1)
    send(1, 1)
    send(1, 2)
    earlier(0, 1)
    lax.fori_loop(0, 2, fold, 0)
    loads[2].wait()
    for piece, (low, number) in enumerate(FAR_PIECES):
        arrive(1, piece)
        if low > 0:
            earlier(1, piece, piece > 0)
        else:
            last()
        if low > 0:
            finish(low, number)

    for stage in range(WIN):
        for piece in range(len(pieces(stage))):
            sent(stage, piece)


def unload(done, waiting, w_out, out, result, sem):
    copies = [
        pltpu.make_async_copy(done.at[half], out.at[0, half, pl.ds(128, GROUP - 128)], sem.at[half])
        for half in range(2)
    ]
    for copy in copies:
        copy.start()
    result[...] = dot(waiting[...], w_out[...]).astype(jnp.bfloat16)
    lasts = [
        pltpu.make_async_copy(
            result.at[pl.ds(half * 128, 128)], out.at[0, half, pl.ds(0, 128)], sem.at[2 + half]
        )
        for half in range(2)
    ]
    for copy in lasts:
        copy.start()
    for copy in copies + lasts:
        copy.wait()


def solution(mesh):
    count = mesh.shape["ctx"]

    def local(frames, episode_lengths, w_qkv, w_out):
        lengths = episode_lengths.reshape(1, -1)
        parts = pl.pallas_call(
            functools.partial(kernel, count),
            out_shape=(
                pltpu.VMEM((2, GROUP - 128, WIDTH), jnp.bfloat16),
                pltpu.VMEM((256, WIDTH), jnp.bfloat16),
                pltpu.VMEM((WIDTH, WIDTH), jnp.bfloat16),
            ),
            in_specs=[
                pl.BlockSpec(memory_space=pltpu.HBM),
                pl.BlockSpec(memory_space=pltpu.HBM),
                pl.BlockSpec(memory_space=pltpu.HBM),
                pl.BlockSpec(memory_space=pltpu.HBM),
            ],
            out_specs=[pl.BlockSpec(memory_space=pltpu.VMEM)] * 3,
            scratch_shapes=[
                pltpu.VMEM((2, GROUP, WIDTH), jnp.bfloat16),
                pltpu.VMEM((2, WIN, GROUP, WIDTH), jnp.bfloat16),
                pltpu.VMEM((WIDTH, 3 * WIDTH), jnp.bfloat16),
                pltpu.VMEM((2 * WIDTH, WIDTH), jnp.bfloat16),
                pltpu.VMEM((2, WIDTH, GROUP), jnp.bfloat16),
                pltpu.VMEM((2, 128, GROUP), jnp.bfloat16),
                pltpu.VMEM((2, 8, GROUP), jnp.float32),
                pltpu.VMEM((2, HEADS, ROWS, GROUP), jnp.float32),
                pltpu.VMEM((8, 128), jnp.float32),
                pltpu.VMEM((2, WIDTH, WIDTH), jnp.bfloat16),
                pltpu.VMEM((2, 128, 128), jnp.float32),
                pltpu.VMEM(lengths.shape, jnp.int32),
                pltpu.SemaphoreType.DMA((4,)),
                pltpu.SemaphoreType.DMA((2, WIN, 3)),
                pltpu.SemaphoreType.DMA((2, WIN, 3)),
            ],
            compiler_params=pltpu.CompilerParams(
                collective_id=0, has_side_effects=True, vmem_limit_bytes=56 * 1024 * 1024
            ),
        )(frames, lengths, w_qkv, w_out)
        return pl.pallas_call(
            unload,
            out_shape=jax.ShapeDtypeStruct(frames.shape, jnp.bfloat16),
            in_specs=[pl.BlockSpec(memory_space=pltpu.VMEM)] * 3,
            out_specs=pl.BlockSpec(memory_space=pltpu.HBM),
            scratch_shapes=[
                pltpu.VMEM((256, WIDTH), jnp.bfloat16),
                pltpu.SemaphoreType.DMA((4,)),
            ],
            compiler_params=pltpu.CompilerParams(vmem_limit_bytes=4 * 1024 * 1024),
        )(*parts)

    in_specs = (P(("dp", "ctx"), None, None, None), P("dp"), P(), P())
    out_specs = P(("dp", "ctx"), None, None, None)
    return jax.shard_map(local, mesh=mesh, in_specs=in_specs, out_specs=out_specs, check_vma=False)
```
